32 devices in a mesh: groups: 2 (over y), learner: 4 (over x, core), tensor: 4 (over z).
Axes of the slice: x: 2, y: 2, z: 4, core: 2. Of those that a mesh axis runs over, the one named last changes fastest.
Arguments:
- hidden: bfloat16 [2, 64, 5120], P(None, ('groups', 'learner')), parts along dimension 1, may hold values from -6 to 6
- input_norm_gain: bfloat16 [5120], replicated, may hold values from 0.5 to 2
- lengths: int32 [64], P(('groups', 'learner')), parts along dimension 0, may hold values from 1 to 1024, as said below
- key_value_cache: bfloat16 [2, 64, 1024, 1024], P(None, ('groups', 'learner'), 'tensor'), parts along dimension 1, may hold values from -512 to 512
- query_base_weight: bfloat16 [5120, 4096], P(None, 'tensor'), may hold values from -0.078125 to 0.078125
- key_value_weight: bfloat16 [2, 5120, 1024], P(None, None, 'tensor'), may hold values from -0.078125 to 0.078125
- output_weight: bfloat16 [4096, 5120], P('tensor'), may hold values from -0.09375 to 0.09375
- adapter_down: bfloat16 [10240, 192], P(('groups', 'learner', 'tensor')), parts along dimension 0, may hold values from -0.078125 to 0.078125
- query_up_factor: bfloat16 [128, 4096], P(('groups', 'learner'), 'tensor'), parts along dimension 0, may hold values from -0.375 to 0.375
- key_value_up: bfloat16 [2, 128, 1024], P(None, ('groups', 'learner'), 'tensor'), parts along dimension 1, may hold values from -0.375 to 0.375
Outputs:
- attended: bfloat16 [2, 64, 5120], P(None, ('groups', 'learner')), parts along dimension 1
- merged_query_weight: bfloat16 [10240, 4096], P('groups', 'tensor'), parts along dimension 0
- kv_merged: bfloat16 [2, 10240, 1024], P(None, 'groups', 'tensor'), parts along dimension 1
The draws below stay inside these ranges and needn't reach their ends.
There are 2 independent parts, one for each index of `groups`. The reference program is written for one: setup_inputs(seed, part) draws one part's arguments, and reference() takes and returns one part's arrays. A program takes and returns all parts, laid end to end along the dimension named above; an argument that names none is the same for every part. Nothing has to cross between parts.
Inputs may be any that keep to these rules, and one draw needn't show every extreme that they name: Row r attends to cache positions below lengths[r]; in every draw some row has exactly 1024.
All inputs are finite; a program needn't handle non-finite values.
Results may differ from the reference program's by a relative error of at most 0.0055.
The reference program's roundings to bfloat16 on the way count: a program that leaves them out, or rounds other values in their place, can miss the bound.
Values may be sent and summed in bfloat16 or wider, within the bound.
A program may use at most 192 MiB of HBM per device.

```python
import math
import jax
import jax.numpy as jnp
from jax import lax

MODEL_DIM = 5120
QUERY_HEADS = 32
KEY_VALUE_HEADS = 8
HEAD_DIM = 128
ADAPTER_RANK = 64
DECODE_STEPS = 2
CACHE_SLOTS = 1024
QD = 4096
KD = 1024
DECODE_ROWS = 32
N_TENSOR = 4


def draw_lengths(key, part):
    key = jax.random.fold_in(key, 11)
    base_key, pick_key = jax.random.split(key)
    drawn = jax.random.randint(base_key, (DECODE_ROWS,), 1, CACHE_SLOTS + 1, dtype=jnp.int32)
    chosen = jax.random.randint(pick_key, (), 0, DECODE_ROWS, dtype=jnp.int32)
    return jnp.where(jnp.arange(DECODE_ROWS, dtype=jnp.int32) == chosen, CACHE_SLOTS, drawn).astype(jnp.int32)


def draw_key_value_cache(key, part):
    key = jax.random.fold_in(key, 23)
    gaussian_key = jax.random.fold_in(key, 0)
    cache_entries = jax.random.normal(gaussian_key, (2, DECODE_ROWS, CACHE_SLOTS, KEY_VALUE_HEADS * HEAD_DIM), jnp.float32)
    return jnp.clip(cache_entries, -512.0, 512.0).astype(jnp.bfloat16)


def level_of(own_key, shape, cuts, low, top_value):
    def one(position, shards_of):
        draws = jax.random.uniform(jax.random.fold_in(jax.random.fold_in(own_key, 6), position), (shards_of,), jnp.float32, low / len(cuts), top_value / len(cuts))
        return jnp.repeat(jnp.exp(draws), shape[position] // shards_of).reshape((-1,) + (1,) * (len(shape) - position - 1))

    gain = one(*cuts[0])
    for cut in cuts[1:]:
        gain = gain * one(*cut)
    return gain


def scatter_about(key, dims, width, bound, cuts=(), kind=jnp.bfloat16):
    values = width * jax.random.normal(key, dims, jnp.float32)
    if cuts:
        values = values * level_of(key, dims, cuts, -0.22, 0.18)
    return jnp.clip(values, -bound, bound).astype(kind)


def setup_inputs(seed: int = 0, part: int = 0) -> dict:
    seeds = jax.random.split(jax.random.key(seed), 11)
    own_keys = jax.random.split(jax.random.fold_in(seeds[10], part), 11)
    return {
        "hidden": scatter_about(own_keys[0], (DECODE_STEPS, DECODE_ROWS, MODEL_DIM), 1.0, 6.0, ((1, 4),)),
        "input_norm_gain": jnp.clip(jnp.exp(jax.random.uniform(seeds[1], (MODEL_DIM,), jnp.float32, math.log(0.5), math.log(2.0))), 0.5, 2.0).astype(jnp.bfloat16),
        "lengths": draw_lengths(jax.random.fold_in(jax.random.fold_in(seeds[10], part), 71), part),
        "key_value_cache": draw_key_value_cache(jax.random.fold_in(jax.random.fold_in(seeds[10], part), 71), part),
        "query_base_weight": scatter_about(seeds[4], (MODEL_DIM, QD), MODEL_DIM ** -0.5, 0.078125, ((1, 4),)),
        "key_value_weight": scatter_about(seeds[5], (2, MODEL_DIM, KD), MODEL_DIM ** -0.5, 0.078125, ((2, 4),)),
        "output_weight": scatter_about(seeds[6], (QD, MODEL_DIM), QD ** -0.5, 0.09375, ((0, 4),)),
        "adapter_down": scatter_about(own_keys[7], (MODEL_DIM, 3 * ADAPTER_RANK), MODEL_DIM ** -0.5, 0.078125, ((0, 16),)),
        "query_up_factor": scatter_about(own_keys[8], (ADAPTER_RANK, QD), (4 * ADAPTER_RANK) ** -0.5, 0.375, ((0, 4), (1, 4))),
        "key_value_up": scatter_about(own_keys[9], (2, ADAPTER_RANK, KD), (4 * ADAPTER_RANK) ** -0.5, 0.375, ((1, 4), (2, 4))),
    }


ADAPTER_SCALE = 2.0
ROPE_BASE = 1000000.0
MASKED_SCORE = -1e+30
NORM_EPSILON = 1e-06

def apply_rotary(values, token_position):
    half_dim = values.shape[-1] // 2
    inverse = ROPE_BASE ** (-jnp.arange(half_dim, dtype=jnp.float32) * 2.0 / values.shape[-1])
    angles = token_position[..., None] * inverse
    cosine = jnp.concatenate([jnp.cos(angles), jnp.cos(angles)], -1)
    sine_table = jnp.concatenate([jnp.sin(angles), jnp.sin(angles)], -1)
    turned = jnp.concatenate([-values[..., half_dim:], values[..., :half_dim]], -1)
    return values * cosine + turned * sine_table

def row_attention(operands):
    key_rows, value_row_list, query_row, fresh_key, fresh_value, length_row = operands
    scale_factor = HEAD_DIM ** (-0.5)
    block_length = CACHE_SLOTS // N_TENSOR
    attention_scores = jnp.einsum('sjgd,pjd->sjgp', query_row.astype(jnp.float32), key_rows.astype(jnp.float32)) * scale_factor
    attention_scores = attention_scores.reshape(DECODE_STEPS, KEY_VALUE_HEADS, QUERY_HEADS // KEY_VALUE_HEADS, N_TENSOR, block_length)
    valid_pos = (jnp.arange(CACHE_SLOTS, dtype=jnp.int32) < length_row).reshape(N_TENSOR, block_length)
    block_max = lax.optimization_barrier(jnp.max(jnp.where(valid_pos, attention_scores, MASKED_SCORE), -1))
    weights = jnp.where(valid_pos, jnp.exp(attention_scores - block_max[..., None]), 0.0)
    totals = lax.optimization_barrier(jnp.sum(weights, -1))
    rounded = lax.optimization_barrier(weights.astype(jnp.bfloat16)).astype(jnp.float32)
    value_blocks = value_row_list.astype(jnp.float32).reshape(N_TENSOR, block_length, KEY_VALUE_HEADS, HEAD_DIM)
    partial_sums = jnp.einsum('sjgbp,bpjd->sjgbd', rounded, value_blocks)
    fresh = jnp.einsum('sjgd,tjd->sjgt', query_row.astype(jnp.float32), fresh_key.astype(jnp.float32)) * scale_factor
    causal = (jnp.arange(DECODE_STEPS)[:, None] >= jnp.arange(DECODE_STEPS)[None, :])[:, None, None, :]
    fresh_top = lax.optimization_barrier(jnp.max(jnp.where(causal, fresh, MASKED_SCORE), -1))
    overall = jnp.maximum(lax.optimization_barrier(jnp.max(block_max, -1)), fresh_top)
    block_weight = jnp.exp(block_max - overall[..., None])
    fresh_weight = jnp.where(causal, jnp.exp(fresh - overall[..., None]), 0.0)
    denominator = lax.optimization_barrier(jnp.sum(totals * block_weight, -1)) + lax.optimization_barrier(jnp.sum(fresh_weight, -1))
    numerator = lax.optimization_barrier(jnp.sum(partial_sums * block_weight[..., None], -2))
    numerator = numerator + jnp.einsum('sjgt,tjd->sjgd', fresh_weight, fresh_value.astype(jnp.float32))
    return (numerator / denominator[..., None]).astype(jnp.bfloat16).reshape(DECODE_STEPS, QUERY_HEADS * HEAD_DIM)

def reference(hidden, input_norm_gain, lengths, key_value_cache, query_base_weight, key_value_weight, output_weight, adapter_down, query_up_factor, key_value_up):
    widened = hidden.astype(jnp.float32)
    normed = (widened * lax.rsqrt(lax.optimization_barrier(jnp.mean(widened * widened, -1, keepdims=True)) + NORM_EPSILON) * input_norm_gain.astype(jnp.float32)).astype(jnp.bfloat16)
    flattened_rows = normed.reshape(DECODE_STEPS * DECODE_ROWS, MODEL_DIM)
    adapter_rank = query_up_factor.shape[0]
    merged_query_weight = (query_base_weight.astype(jnp.float32) + ADAPTER_SCALE * jnp.dot(adapter_down[:, :adapter_rank], query_up_factor, preferred_element_type=jnp.float32)).astype(jnp.bfloat16)
    merged_key_weight = (key_value_weight[0].astype(jnp.float32) + ADAPTER_SCALE * jnp.dot(adapter_down[:, adapter_rank:2 * adapter_rank], key_value_up[0], preferred_element_type=jnp.float32)).astype(jnp.bfloat16)
    merged_value_weight = (key_value_weight[1].astype(jnp.float32) + ADAPTER_SCALE * jnp.dot(adapter_down[:, 2 * adapter_rank:], key_value_up[1], preferred_element_type=jnp.float32)).astype(jnp.bfloat16)
    token_position = (lengths[None, :] + jnp.arange(DECODE_STEPS, dtype=jnp.int32)[:, None]).astype(jnp.float32)
    query_proj = jnp.dot(flattened_rows, merged_query_weight, preferred_element_type=jnp.float32).reshape(DECODE_STEPS, DECODE_ROWS, QUERY_HEADS, HEAD_DIM)
    query_vectors = apply_rotary(query_proj, token_position[:, :, None]).astype(jnp.bfloat16)
    key_projected = lax.optimization_barrier(jnp.dot(flattened_rows, merged_key_weight, preferred_element_type=jnp.float32).astype(jnp.bfloat16))
    current_keys = apply_rotary(key_projected.astype(jnp.float32).reshape(DECODE_STEPS, DECODE_ROWS, KEY_VALUE_HEADS, HEAD_DIM), token_position[:, :, None]).astype(jnp.bfloat16)
    current_values = jnp.dot(flattened_rows, merged_value_weight, preferred_element_type=jnp.float32).astype(jnp.bfloat16).reshape(DECODE_STEPS, DECODE_ROWS, KEY_VALUE_HEADS, HEAD_DIM)
    grouped_queries = query_vectors.reshape(DECODE_STEPS, DECODE_ROWS, KEY_VALUE_HEADS, QUERY_HEADS // KEY_VALUE_HEADS, HEAD_DIM)
    attention_result = lax.map(row_attention, (key_value_cache[0].reshape(DECODE_ROWS, CACHE_SLOTS, KEY_VALUE_HEADS, HEAD_DIM), key_value_cache[1].reshape(DECODE_ROWS, CACHE_SLOTS, KEY_VALUE_HEADS, HEAD_DIM), jnp.swapaxes(grouped_queries, 0, 1), jnp.swapaxes(current_keys, 0, 1), jnp.swapaxes(current_values, 0, 1), lengths))
    attention_result = jnp.swapaxes(attention_result, 0, 1).reshape(DECODE_STEPS * DECODE_ROWS, QUERY_HEADS * HEAD_DIM)
    attended = jnp.dot(attention_result, output_weight, preferred_element_type=jnp.float32).astype(jnp.bfloat16)
    kv_merged = jnp.stack([merged_key_weight, merged_value_weight])
    return (attended.reshape(DECODE_STEPS, DECODE_ROWS, MODEL_DIM), merged_query_weight, kv_merged)
```

```python
import math
import jax
import jax.numpy as jnp
from jax import lax
from jax.experimental import pallas as pl
from jax.experimental.pallas import tpu as pltpu
from jax.sharding import PartitionSpec as P

QUERY_HEADS = 32
KEY_VALUE_HEADS = 8
HEAD_DIM = 128
MESH = pl.DeviceIdType.MESH


ADAPTER_SCALE = 2.0
ROPE_BASE = 1000000.0
MASKED_SCORE = -1e30
NORM_EPSILON = 1e-06


def joined(part, axis, combine):
    gathered = jax.tree.map(lambda a: lax.all_gather(a, axis), part)

    def take(source):
        return jax.tree.map(lambda a: lax.dynamic_index_in_dim(a, source, 0, False), gathered)

    return lax.fori_loop(
        1, lax.axis_size(axis), lambda source, state: combine(state, take(source)), take(0)
    )


def apply_rotary(values, token_position):
    half_dim = values.shape[-1] // 2
    inverse = ROPE_BASE ** (-jnp.arange(half_dim, dtype=jnp.float32) * 2.0 / values.shape[-1])
    angles = token_position[..., None] * inverse
    cosine = jnp.concatenate([jnp.cos(angles), jnp.cos(angles)], -1)
    sine_table = jnp.concatenate([jnp.sin(angles), jnp.sin(angles)], -1)
    turned = jnp.concatenate([-values[..., half_dim:], values[..., :half_dim]], -1)
    return values * cosine + turned * sine_table


def combine_pair(former, latter):
    highest = jnp.maximum(former[0], latter[0])
    former_scale = jnp.exp(former[0] - highest)
    latter_scale = jnp.exp(latter[0] - highest)
    return (
        highest,
        former[1] * former_scale + latter[1] * latter_scale,
        former[2] * former_scale[..., None] + latter[2] * latter_scale[..., None],
    )


def per_device(
    hidden,
    input_norm_gain,
    lengths,
    key_value_cache,
    query_base_weight,
    key_value_weight,
    output_weight,
    adapter_down,
    query_up_factor,
    key_value_up,
):
    step_total, row_total, model_width = hidden.shape
    group_width = QUERY_HEADS // KEY_VALUE_HEADS
    tensor_rank = lax.axis_index("tensor")
    local_cols = query_base_weight.shape[1]
    local_heads = local_cols // HEAD_DIM
    widened = hidden.astype(jnp.float32)
    normed = (
        widened
        * lax.rsqrt(jnp.mean(widened * widened, -1, keepdims=True) + NORM_EPSILON)
        * input_norm_gain.astype(jnp.float32)
    ).astype(jnp.bfloat16)
    flattened_rows = normed.reshape(step_total * row_total, model_width)
    query_delta, key_value_delta = (
        lax.all_gather(query_up_factor, "learner", axis=0, tiled=True),
        lax.all_gather(key_value_up, "learner", axis=1, tiled=True),
    )
    adapter_rank = query_delta.shape[0]
    down_slice = lax.all_gather(adapter_down, ("learner", "tensor"), axis=0, tiled=True)
    query_rows = (
        query_base_weight.astype(jnp.float32)
        + ADAPTER_SCALE
        * jnp.dot(down_slice[:, :adapter_rank], query_delta, preferred_element_type=jnp.float32)
    ).astype(jnp.bfloat16)
    key_rows = (
        key_value_weight[0].astype(jnp.float32)
        + ADAPTER_SCALE
        * jnp.dot(
            down_slice[:, adapter_rank : 2 * adapter_rank],
            key_value_delta[0],
            preferred_element_type=jnp.float32,
        )
    ).astype(jnp.bfloat16)
    value_row_list = (
        key_value_weight[1].astype(jnp.float32)
        + ADAPTER_SCALE
        * jnp.dot(
            down_slice[:, 2 * adapter_rank :],
            key_value_delta[1],
            preferred_element_type=jnp.float32,
        )
    ).astype(jnp.bfloat16)
    query_sum = jnp.dot(flattened_rows, query_rows, preferred_element_type=jnp.float32)
    key_sum = jnp.dot(flattened_rows, key_rows, preferred_element_type=jnp.float32)
    value_sum = jnp.dot(flattened_rows, value_row_list, preferred_element_type=jnp.float32)
    merged_query_weight = query_rows
    kv_merged = jnp.stack([key_rows, value_row_list])
    query_sum, key_sum, value_sum, merged_query_weight, kv_merged = (
        query_sum,
        key_sum,
        value_sum,
        merged_query_weight,
        kv_merged,
    )
    token_position = (lengths[None, :] + jnp.arange(step_total, dtype=jnp.int32)[:, None]).astype(
        jnp.float32
    )
    own_query = apply_rotary(
        query_sum.reshape(step_total, row_total, local_heads, HEAD_DIM), token_position[:, :, None]
    ).astype(jnp.bfloat16)
    query_heads_all, key_all, value_heads_all = (
        lax.all_gather(
            own_query.reshape(step_total * row_total, local_cols), "tensor", axis=1, tiled=True
        ),
        lax.all_gather(key_sum.astype(jnp.bfloat16), "tensor", axis=1, tiled=True),
        lax.all_gather(value_sum.astype(jnp.bfloat16), "tensor", axis=1, tiled=True),
    )
    current_keys = apply_rotary(
        lax.optimization_barrier(key_all)
        .astype(jnp.float32)
        .reshape(step_total, row_total, KEY_VALUE_HEADS, HEAD_DIM),
        token_position[:, :, None],
    ).astype(jnp.bfloat16)
    current_values = value_heads_all.reshape(step_total, row_total, KEY_VALUE_HEADS, HEAD_DIM)
    grouped_queries = query_heads_all.reshape(
        step_total, row_total, KEY_VALUE_HEADS, group_width, HEAD_DIM
    )
    block_length = key_value_cache.shape[2]
    stored_keys = key_value_cache[0].reshape(row_total, block_length, KEY_VALUE_HEADS, HEAD_DIM)
    stored_values = key_value_cache[1].reshape(row_total, block_length, KEY_VALUE_HEADS, HEAD_DIM)
    scale_factor = HEAD_DIM ** (-0.5)
    places = tensor_rank * block_length + jnp.arange(block_length, dtype=jnp.int32)
    valid_pos = (places[None, :] < lengths[:, None])[None, :, None, None, :]
    attention_scores = (
        jnp.einsum(
            "srjgd,rpjd->srjgp", grouped_queries, stored_keys, preferred_element_type=jnp.float32
        )
        * scale_factor
    )
    block_max = jnp.max(jnp.where(valid_pos, attention_scores, MASKED_SCORE), -1)
    weights = jnp.where(valid_pos, jnp.exp(attention_scores - block_max[..., None]), 0.0)
    totals = jnp.sum(weights, -1)
    numer_block = jnp.einsum(
        "srjgp,rpjd->srjgd",
        weights.astype(jnp.bfloat16),
        stored_values,
        preferred_element_type=jnp.float32,
    )
    block_max = block_max.reshape(step_total, row_total, QUERY_HEADS)
    totals = totals.reshape(step_total, row_total, QUERY_HEADS)
    numer_block = numer_block.reshape(step_total, row_total, QUERY_HEADS, HEAD_DIM)
    first_head = tensor_rank * local_heads
    full_max, full_total, full_numer = joined(
        (block_max, totals, numer_block), "tensor", combine_pair
    )
    cache_max = lax.dynamic_slice_in_dim(full_max, first_head, local_heads, 2)
    cache_total = lax.dynamic_slice_in_dim(full_total, first_head, local_heads, 2)
    cache_numer = lax.dynamic_slice_in_dim(full_numer, first_head, local_heads, 2)
    own_keys = lax.dynamic_slice_in_dim(
        jnp.repeat(current_keys, group_width, axis=2), first_head, local_heads, 2
    )
    own_values = lax.dynamic_slice_in_dim(
        jnp.repeat(current_values, group_width, axis=2), first_head, local_heads, 2
    )
    fresh = (
        jnp.einsum("srhd,trhd->srht", own_query, own_keys, preferred_element_type=jnp.float32)
        * scale_factor
    )
    causal = (jnp.arange(step_total)[:, None] >= jnp.arange(step_total)[None, :])[:, None, None, :]
    overall = jnp.maximum(cache_max, jnp.max(jnp.where(causal, fresh, MASKED_SCORE), -1))
    cache_weight = jnp.exp(cache_max - overall)
    fresh_weight = jnp.where(causal, jnp.exp(fresh - overall[..., None]), 0.0)
    denominator = cache_total * cache_weight + jnp.sum(fresh_weight, -1)
    numerator = cache_numer * cache_weight[..., None] + jnp.einsum(
        "srht,trhd->srhd", fresh_weight, own_values.astype(jnp.float32)
    )
    attention_result = (
        (numerator / denominator[..., None])
        .astype(jnp.bfloat16)
        .reshape(step_total * row_total, local_cols)
    )
    partial_out = jnp.dot(attention_result, output_weight, preferred_element_type=jnp.float32)
    attended = lax.psum(partial_out, "tensor").astype(jnp.bfloat16)
    return (attended.reshape(step_total, row_total, model_width), merged_query_weight, kv_merged)


def gather_kernel(
    hidden_ref, gain_ref, down_ref, upq_ref, upkv_ref,
    pall_ref, uq_ref, uk_ref, uv_ref, nb_ref,
    pk, upq_g, upkv_g, up_send, up_recv, b_send, b_recv, own_sem,
):
    f32, bf16 = jnp.float32, jnp.bfloat16
    L, T = 4, 4
    l, t = lax.axis_index("learner"), lax.axis_index("tensor")
    tp = [lax.rem(t + d, T) for d in range(T)]
    lp = [lax.rem(l + d, L) for d in range(L)]
    barrier = pltpu.get_barrier_semaphore()
    for d in range(1, 4):
        pl.semaphore_signal(barrier, inc=1, device_id={"tensor": tp[d]}, device_id_type=MESH)
        pl.semaphore_signal(barrier, inc=1, device_id={"learner": lp[d]}, device_id_type=MESH)
    shard = down_ref[...]
    rows = shard.shape[0]
    half = rows // 2
    pk[0:rows, :] = shard[:, :128]
    pk[rows : rows + half, :] = jnp.concatenate([shard[:half, 128:], shard[half:, 128:]], axis=1)
    pl.semaphore_wait(barrier, 6)

    waits = []
    l2 = lax.rem(l + 2, L)
    l1 = l + 1 - 2 * lax.rem(l, 2)
    l3 = lax.rem(l1 + 2, L)
    t1 = t + 1 - 2 * lax.rem(t, 2)
    zp = [t, t1, lax.rem(t + 2, T), lax.rem(t1 + 2, T)]

    def bulk(src, blk, dev):
        c = pltpu.make_async_remote_copy(
            src_ref=src, dst_ref=pall_ref.at[blk], send_sem=b_send.at[len(waits)], recv_sem=b_recv.at[blk],
            device_id=dev, device_id_type=MESH,
        )
        c.start()
        waits.append(c)

    def arrived(blk):
        pltpu.make_async_remote_copy(
            src_ref=pk, dst_ref=pall_ref.at[blk], send_sem=b_send.at[0], recv_sem=b_recv.at[blk],
            device_id={"tensor": t1}, device_id_type=MESH,
        ).wait_recv()

    b = l * T + t
    bulk(pk, b, {"learner": l2})
    for k in (1, 2, 3):
        bulk(pk, b, {"tensor": zp[k]})
    bulk(pk, b, {"learner": l1})
    own = pltpu.make_async_copy(pk, pall_ref.at[b], own_sem)
    own.start()
    ups = []
    for d in range(1, 4):
        for k, (src, dst) in enumerate(((upq_ref, upq_g), (upkv_ref, upkv_g))):
            c = pltpu.make_async_remote_copy(
                src_ref=src, dst_ref=dst.at[l], send_sem=up_send.at[k, d], recv_sem=up_recv.at[k, d],
                device_id={"learner": lp[d]}, device_id_type=MESH,
            )
            c.start()
            ups.append(c)
    upq_g[l] = upq_ref[...]
    upkv_g[l] = upkv_ref[...]

    model = gain_ref.shape[1]
    wide = hidden_ref[...].astype(f32).reshape(16, model)
    inv = lax.rsqrt(jnp.mean(wide * wide, -1, keepdims=True) + NORM_EPSILON)
    normed = (wide * inv * gain_ref[...].astype(f32)).astype(bf16)
    wid = nb_ref.shape[2]
    for k in range(nb_ref.shape[0]):
        nb_ref[k] = normed[:, k * wid : (k + 1) * wid]
    uq_ref[...] = jnp.zeros_like(uq_ref)
    uk_ref[...] = jnp.zeros_like(uk_ref)
    uv_ref[...] = jnp.zeros_like(uv_ref)

    for k in (1, 2, 3):
        blk = l * T + zp[k]
        arrived(blk)
        bulk(pall_ref.at[blk], blk, {"learner": l2})
        bulk(pall_ref.at[blk], blk, {"learner": l1})
        blk = l2 * T + zp[k - 1]
        arrived(blk)
        bulk(pall_ref.at[blk], blk, {"learner": l1})
    for c in ups:
        c.wait_recv()
    uq_ref[0:64, :] = upq_g[...].reshape(64, upq_g.shape[2])
    kvg = upkv_g[...]
    uk_ref[64:128, :] = kvg[:, 0].reshape(64, upkv_g.shape[3])
    uv_ref[64:128, :] = kvg[:, 1].reshape(64, upkv_g.shape[3])
    blk = l2 * T + zp[3]
    arrived(blk)
    bulk(pall_ref.at[blk], blk, {"learner": l1})
    for k in range(4):
        arrived(l1 * T + k)
        arrived(l3 * T + k)
    own.wait()
    for c in ups + waits:
        c.wait_send()


def merge_kernel(
    p_ref, uq_ref, uk_ref, uv_ref, n_ref, wq_ref, wkv_ref, oq_ref, okv_ref, qs_ref, ks_ref, vs_ref
):
    f32, bf16 = jnp.float32, jnp.bfloat16
    rows = p_ref.shape[1] * 2 // 3
    half = rows // 2

    @pl.when(pl.program_id(0) == 0)
    def _():
        qs_ref[...] = jnp.zeros_like(qs_ref)
        ks_ref[...] = jnp.zeros_like(ks_ref)
        vs_ref[...] = jnp.zeros_like(vs_ref)

    uv_high = uv_ref[...]
    uv_low = jnp.concatenate([uv_high[64:], uv_high[:64]], axis=0)
    for e in range(p_ref.shape[0]):
        p = p_ref[e]
        qk, pv = p[:rows], p[rows:]
        cut = slice(e * rows, (e + 1) * rows)
        dq = jnp.dot(qk, uq_ref[...], preferred_element_type=f32)
        oq_ref[cut] = (wq_ref[cut].astype(f32) + ADAPTER_SCALE * dq).astype(bf16)
        dk = jnp.dot(qk, uk_ref[...], preferred_element_type=f32)
        okv_ref[0, cut] = (wkv_ref[0, cut].astype(f32) + ADAPTER_SCALE * dk).astype(bf16)
        for k, up in enumerate((uv_low, uv_high)):
            dv = jnp.dot(pv, up, preferred_element_type=f32)
            cut = slice(e * rows + k * half, e * rows + (k + 1) * half)
            okv_ref[1, cut] = (wkv_ref[1, cut].astype(f32) + ADAPTER_SCALE * dv).astype(bf16)
    n = n_ref[0]
    qs_ref[...] += jnp.dot(n, oq_ref[...], preferred_element_type=f32)
    ks_ref[...] += jnp.dot(n, okv_ref[0], preferred_element_type=f32)
    vs_ref[...] += jnp.dot(n, okv_ref[1], preferred_element_type=f32)


def decode_kernel(
    lengths_ref, qs_ref, ks_ref, vs_ref, cache_hbm, wo_hbm,
    att_ref,
    kc, vc, wo,
    qtmp, qall, keyf, valf, nsend, nrecv, msend, mrecv, res, abuf,
    psend, precv, asend, arecv,
    load_sem, q_send, q_recv, n_send, n_recv, m_send, m_recv, p_send, p_recv, a_send, a_recv,
):
    f32, bf16 = jnp.float32, jnp.bfloat16
    T = 4
    t = lax.axis_index("tensor")
    model = wo.shape[1]
    scale = HEAD_DIM ** (-0.5)
    tp = [lax.rem(t + d, T) for d in range(T)]

    def to_t(d):
        return {"tensor": tp[d]}

    barrier = pltpu.get_barrier_semaphore()
    for d in range(1, 4):
        pl.semaphore_signal(barrier, inc=1, device_id=to_t(d), device_id_type=MESH)
    loads = [
        pltpu.make_async_copy(cache_hbm.at[0], kc, load_sem.at[0]),
        pltpu.make_async_copy(cache_hbm.at[1], vc, load_sem.at[1]),
        pltpu.make_async_copy(wo_hbm, wo, load_sem.at[2]),
    ]
    for c in loads:
        c.start()
    waits = []

    def send(src, dst, ssem, rsem, dev):
        c = pltpu.make_async_remote_copy(
            src_ref=src, dst_ref=dst, send_sem=ssem, recv_sem=rsem, device_id=dev, device_id_type=MESH
        )
        c.start()
        waits.append(c)
        return c

    sub = lax.broadcasted_iota(jnp.int32, (16, 128), 0)
    lane = lax.broadcasted_iota(jnp.int32, (16, 128), 1)
    row = lax.rem(sub, 8)
    pos = jnp.zeros((16, 128), jnp.int32)
    for r in range(8):
        pos = jnp.where(row == r, lengths_ref[r], pos)
    pos = (pos + jnp.where(sub >= 8, 1, 0)).astype(f32)
    freq = jnp.exp(lax.rem(lane, 64).astype(f32) * (-2.0 / HEAD_DIM * math.log(ROPE_BASE)))
    cosine = jnp.cos(pos * freq)
    sine = jnp.sin(pos * freq)
    sine = jnp.where(lane < 64, -sine, sine)

    def rope(v):
        return v * cosine + pltpu.roll(v, 64, 1) * sine

    qacc = qs_ref[...]
    kacc = ks_ref[...].astype(bf16).astype(f32)
    valf[...] = vs_ref[...].astype(bf16).astype(f32)
    pl.semaphore_wait(barrier, 3)

    for h in range(8):
        v = rope(qacc[:, h * 128 : (h + 1) * 128])
        for s in range(2):
            start = (h // 4) * 8 + s * 4 + h % 4
            qtmp[pl.ds(start, 8, stride=16), :] = v[s * 8 : (s + 1) * 8, :]
    qall[0] = qtmp[...].astype(bf16)
    qs = [send(qall.at[0], qall.at[d], q_send.at[d], q_recv.at[d], to_t(d)) for d in range(1, 4)]
    for h in range(2):
        keyf[:, h * 128 : (h + 1) * 128] = rope(kacc[:, h * 128 : (h + 1) * 128]).astype(bf16).astype(f32)

    loads[0].wait()
    loads[1].wait()
    first = sub[:, 0:1] < 8
    place = t * kc.shape[1] + lax.broadcasted_iota(jnp.int32, (16, kc.shape[1]), 1)
    lane2 = lane
    ns_copies = [None] * 4
    per = 4

    def attend(d):
        owner = lax.rem(t + T - d, T)
        cols = pl.multiple_of(owner * 256, 256)

        def step(i, ml):
            for u in range(per):
                r = i * per + u
                q16 = qall[d, pl.ds(pl.multiple_of(r * 16, 16), 16), :]
                kk = kc[r, :, pl.ds(cols, 256)]
                vv = vc[r, :, pl.ds(cols, 256)]
                dims = (((1,), (1,)), ((), ()))
                s0 = lax.dot_general(q16, kk[:, :128], dims, preferred_element_type=f32)
                s1 = lax.dot_general(q16, kk[:, 128:], dims, preferred_element_type=f32)
                s = jnp.where(first, s0, s1) * scale
                valid = place < lengths_ref[r]
                m = jnp.max(jnp.where(valid, s, MASKED_SCORE), -1, keepdims=True)
                w = jnp.where(valid, jnp.exp(s - m), 0.0)
                tot = jnp.sum(w, -1, keepdims=True)
                nn = jnp.dot(w.astype(bf16), vv, preferred_element_type=f32)
                nn = jnp.where(first, nn[:, :128], nn[:, 128:])
                nsend[d, pl.ds(pl.multiple_of(r * 16, 16), 16), :] = nn.astype(nsend.dtype)
                ml = jnp.where(lane2 == r, m, jnp.where(lane2 == r + 8, tot, ml))
            return ml

        msend[d] = lax.fori_loop(0, 8 // per, step, jnp.zeros((16, 128), f32))

    attend(0)
    nsc, msc = [], []
    for d in range(1, 4):
        qs[d - 1].wait_recv()
        attend(d)
        back = 4 - d
        nsc.append(send(nsend.at[d], nrecv.at[back], n_send.at[d], n_recv.at[back], to_t(back)))
        msc.append(send(msend.at[d], mrecv.at[back], m_send.at[d], m_recv.at[back], to_t(back)))

    for c in nsc:
        c.wait_recv()
    for c in msc:
        c.wait_recv()
    nrecv[0] = nsend[0]
    mrecv[0] = msend[0]
    late = lax.rem(sub[:, 0:1] // 4, 2) == 1
    for r in range(8):
        q16 = qall[0, r * 16 : (r + 1) * 16, :].astype(f32)
        fresh = []
        vals = []
        for u in range(2):
            k16 = jnp.where(first, keyf[u * 8 + r : u * 8 + r + 1, 0:128], keyf[u * 8 + r : u * 8 + r + 1, 128:256])
            vals.append(
                jnp.where(first, valf[u * 8 + r : u * 8 + r + 1, 0:128], valf[u * 8 + r : u * 8 + r + 1, 128:256])
            )
            fresh.append(jnp.sum(q16 * k16, -1, keepdims=True) * scale)
        fresh[1] = jnp.where(late, fresh[1], MASKED_SCORE)
        ms = [mrecv[d, :, r : r + 1] for d in range(4)]
        top = jnp.maximum(fresh[0], fresh[1])
        for m in ms:
            top = jnp.maximum(top, m)
        w0 = jnp.exp(fresh[0] - top)
        w1 = jnp.where(late, jnp.exp(fresh[1] - top), 0.0)
        den = w0 + w1
        num = w0 * vals[0] + w1 * vals[1]
        for d in range(4):
            e = jnp.exp(ms[d] - top)
            den = den + e * mrecv[d, :, 8 + r : 9 + r]
            num = num + e * nrecv[d, r * 16 : (r + 1) * 16, :].astype(f32)
        res[r * 16 : (r + 1) * 16, :] = num / den
    for h in range(8):
        for s in range(2):
            start = (h // 4) * 8 + s * 4 + h % 4
            abuf[s * 8 : (s + 1) * 8, h * 128 : (h + 1) * 128] = res[pl.ds(start, 8, stride=16), :]
    a = abuf[...].astype(bf16)

    loads[2].wait()
    quarter = model // T
    ps = []
    for d in (2, 1, 3):
        o = jnp.dot(a, wo[:, pl.ds(pl.multiple_of(tp[d] * quarter, 128), quarter)], preferred_element_type=f32)
        psend[d] = o.astype(bf16)
        ps.append(send(psend.at[d], precv.at[d], p_send.at[d], p_recv.at[d], to_t(d)))
    total = jnp.dot(a, wo[:, pl.ds(pl.multiple_of(t * quarter, 128), quarter)], preferred_element_type=f32)

    for c in ps:
        c.wait_recv()
    for d in range(1, 4):
        total = total + precv[d].astype(f32)
    asend[...] = total.astype(bf16)
    acs = [send(asend, arecv.at[t], a_send.at[d], a_recv.at[d], to_t(d)) for d in range(1, 4)]
    arecv[t] = asend[...]
    for c in acs:
        c.wait_recv()
    for k in range(4):
        both = arecv[k].astype(f32)
        for s in range(2):
            att_ref[s, :, k * quarter : (k + 1) * quarter] = both[s * 8 : (s + 1) * 8, :].astype(bf16)
    for c in waits:
        c.wait_send()


def fused_device(
    hidden, input_norm_gain, lengths, key_value_cache, query_base_weight, key_value_weight,
    output_weight, adapter_down, query_up_factor, key_value_up,
):
    f32, bf16 = jnp.float32, jnp.bfloat16
    model = hidden.shape[2]
    part = model // 4
    rows = adapter_down.shape[0]
    packed = rows + rows // 2
    steps = 8
    V, A, S = pltpu.VMEM, pl.ANY, pltpu.SMEM
    dma = pltpu.SemaphoreType.DMA
    spec = lambda m: pl.BlockSpec(memory_space=m)
    shape = jax.ShapeDtypeStruct
    p_all, uq, uk, uv, blocks = pl.pallas_call(
        gather_kernel,
        out_shape=[
            shape((16, packed, 128), bf16), shape((128, 1024), bf16), shape((128, 256), bf16),
            shape((128, 256), bf16), shape((steps, 16, model // steps), bf16),
        ],
        in_specs=[spec(V)] * 5,
        out_specs=[spec(A)] + [spec(V)] * 4,
        scratch_shapes=[
            V((packed, 128), bf16), V((4, 16, 1024), bf16), V((4, 2, 16, 256), bf16),
            dma((2, 4)), dma((2, 4)), dma((15,)), dma((16,)), dma,
        ],
        compiler_params=pltpu.CompilerParams(
            collective_id=0, has_side_effects=True, vmem_limit_bytes=32 * 1024 * 1024
        ),
        name="gather",
    )(hidden, input_norm_gain.reshape(1, model), adapter_down, query_up_factor, key_value_up)
    wide = model // steps
    whole = lambda *sh: pl.BlockSpec(sh, lambda i: (0,) * len(sh))
    merged, kv_merged, qs, ks, vs = pl.pallas_call(
        merge_kernel,
        grid=(steps,),
        out_shape=[
            shape(query_base_weight.shape, bf16), shape(key_value_weight.shape, bf16),
            shape((16, 1024), f32), shape((16, 256), f32), shape((16, 256), f32),
        ],
        in_specs=[
            pl.BlockSpec((16 // steps, packed, 128), lambda i: (i, 0, 0)),
            whole(128, 1024), whole(128, 256), whole(128, 256),
            pl.BlockSpec((1, 16, wide), lambda i: (i, 0, 0)),
            pl.BlockSpec((wide, 1024), lambda i: (i, 0)),
            pl.BlockSpec((2, wide, 256), lambda i: (0, i, 0)),
        ],
        out_specs=[
            pl.BlockSpec((wide, 1024), lambda i: (i, 0)),
            pl.BlockSpec((2, wide, 256), lambda i: (0, i, 0)),
            whole(16, 1024), whole(16, 256), whole(16, 256),
        ],
        compiler_params=pltpu.CompilerParams(vmem_limit_bytes=40 * 1024 * 1024),
        name="merge",
    )(p_all, uq, uk, uv, blocks, query_base_weight, key_value_weight)
    attended = pl.pallas_call(
        decode_kernel,
        out_shape=shape(hidden.shape, bf16),
        in_specs=[spec(S)] + [spec(V)] * 3 + [spec(A)] * 2,
        out_specs=spec(V),
        scratch_shapes=[
            V((8, 256, 1024), bf16), V((8, 256, 1024), bf16), V((1024, model), bf16),
            V((128, 128), f32), V((4, 128, 128), bf16), V((16, 256), f32), V((16, 256), f32),
            V((4, 128, 128), bf16), V((4, 128, 128), bf16), V((4, 16, 128), f32), V((4, 16, 128), f32),
            V((128, 128), f32), V((16, 1024), f32),
            V((4, 16, part), bf16), V((4, 16, part), bf16), V((16, part), bf16), V((4, 16, part), bf16),
            dma((3,)),
        ]
        + [dma((4,))] * 10,
        compiler_params=pltpu.CompilerParams(
            collective_id=1, has_side_effects=True, vmem_limit_bytes=48 * 1024 * 1024
        ),
        name="decode",
    )(lengths, qs, ks, vs, key_value_cache, output_weight)
    return attended, merged, kv_merged


def solution(mesh):
    small = mesh.shape["learner"] == 4 and mesh.shape["tensor"] == 4
    return jax.shard_map(
        fused_device if small else per_device,
        mesh=mesh,
        in_specs=(
            P(None, ("groups", "learner"), None),
            P(),
            P(("groups", "learner")),
            P(None, ("groups", "learner"), "tensor", None),
            P(None, "tensor"),
            P(None, None, "tensor"),
            P("tensor", None),
            P(("groups", "learner", "tensor"), None),
            P(("groups", "learner"), "tensor"),
            P(None, ("groups", "learner"), "tensor"),
        ),
        out_specs=(
            P(None, ("groups", "learner"), None),
            P("groups", "tensor"),
            P(None, "groups", "tensor"),
        ),
        check_vma=False,
    )
```

```python
import math
import jax
import jax.numpy as jnp
from jax import lax
from jax.experimental import pallas as pl
from jax.experimental.pallas import tpu as pltpu
from jax.sharding import PartitionSpec as P

QUERY_HEADS = 32
KEY_VALUE_HEADS = 8
HEAD_DIM = 128
MESH = pl.DeviceIdType.MESH


ADAPTER_SCALE = 2.0
ROPE_BASE = 1000000.0
MASKED_SCORE = -1e30
NORM_EPSILON = 1e-06


def joined(part, axis, combine):
    gathered = jax.tree.map(lambda a: lax.all_gather(a, axis), part)

    def take(source):
        return jax.tree.map(lambda a: lax.dynamic_index_in_dim(a, source, 0, False), gathered)

    return lax.fori_loop(
        1, lax.axis_size(axis), lambda source, state: combine(state, take(source)), take(0)
    )


def apply_rotary(values, token_position):
    half_dim = values.shape[-1] // 2
    inverse = ROPE_BASE ** (-jnp.arange(half_dim, dtype=jnp.float32) * 2.0 / values.shape[-1])
    angles = token_position[..., None] * inverse
    cosine = jnp.concatenate([jnp.cos(angles), jnp.cos(angles)], -1)
    sine_table = jnp.concatenate([jnp.sin(angles), jnp.sin(angles)], -1)
    turned = jnp.concatenate([-values[..., half_dim:], values[..., :half_dim]], -1)
    return values * cosine + turned * sine_table


def combine_pair(former, latter):
    highest = jnp.maximum(former[0], latter[0])
    former_scale = jnp.exp(former[0] - highest)
    latter_scale = jnp.exp(latter[0] - highest)
    return (
        highest,
        former[1] * former_scale + latter[1] * latter_scale,
        former[2] * former_scale[..., None] + latter[2] * latter_scale[..., None],
    )


def per_device(
    hidden,
    input_norm_gain,
    lengths,
    key_value_cache,
    query_base_weight,
    key_value_weight,
    output_weight,
    adapter_down,
    query_up_factor,
    key_value_up,
):
    step_total, row_total, model_width = hidden.shape
    group_width = QUERY_HEADS // KEY_VALUE_HEADS
    tensor_rank = lax.axis_index("tensor")
    local_cols = query_base_weight.shape[1]
    local_heads = local_cols // HEAD_DIM
    widened = hidden.astype(jnp.float32)
    normed = (
        widened
        * lax.rsqrt(jnp.mean(widened * widened, -1, keepdims=True) + NORM_EPSILON)
        * input_norm_gain.astype(jnp.float32)
    ).astype(jnp.bfloat16)
    flattened_rows = normed.reshape(step_total * row_total, model_width)
    query_delta, key_value_delta = (
        lax.all_gather(query_up_factor, "learner", axis=0, tiled=True),
        lax.all_gather(key_value_up, "learner", axis=1, tiled=True),
    )
    adapter_rank = query_delta.shape[0]
    down_slice = lax.all_gather(adapter_down, ("learner", "tensor"), axis=0, tiled=True)
    query_rows = (
        query_base_weight.astype(jnp.float32)
        + ADAPTER_SCALE
        * jnp.dot(down_slice[:, :adapter_rank], query_delta, preferred_element_type=jnp.float32)
    ).astype(jnp.bfloat16)
    key_rows = (
        key_value_weight[0].astype(jnp.float32)
        + ADAPTER_SCALE
        * jnp.dot(
            down_slice[:, adapter_rank : 2 * adapter_rank],
            key_value_delta[0],
            preferred_element_type=jnp.float32,
        )
    ).astype(jnp.bfloat16)
    value_row_list = (
        key_value_weight[1].astype(jnp.float32)
        + ADAPTER_SCALE
        * jnp.dot(
            down_slice[:, 2 * adapter_rank :],
            key_value_delta[1],
            preferred_element_type=jnp.float32,
        )
    ).astype(jnp.bfloat16)
    query_sum = jnp.dot(flattened_rows, query_rows, preferred_element_type=jnp.float32)
    key_sum = jnp.dot(flattened_rows, key_rows, preferred_element_type=jnp.float32)
    value_sum = jnp.dot(flattened_rows, value_row_list, preferred_element_type=jnp.float32)
    merged_query_weight = query_rows
    kv_merged = jnp.stack([key_rows, value_row_list])
    query_sum, key_sum, value_sum, merged_query_weight, kv_merged = (
        query_sum,
        key_sum,
        value_sum,
        merged_query_weight,
        kv_merged,
    )
    token_position = (lengths[None, :] + jnp.arange(step_total, dtype=jnp.int32)[:, None]).astype(
        jnp.float32
    )
    own_query = apply_rotary(
        query_sum.reshape(step_total, row_total, local_heads, HEAD_DIM), token_position[:, :, None]
    ).astype(jnp.bfloat16)
    query_heads_all, key_all, value_heads_all = (
        lax.all_gather(
            own_query.reshape(step_total * row_total, local_cols), "tensor", axis=1, tiled=True
        ),
        lax.all_gather(key_sum.astype(jnp.bfloat16), "tensor", axis=1, tiled=True),
        lax.all_gather(value_sum.astype(jnp.bfloat16), "tensor", axis=1, tiled=True),
    )
    current_keys = apply_rotary(
        lax.optimization_barrier(key_all)
        .astype(jnp.float32)
        .reshape(step_total, row_total, KEY_VALUE_HEADS, HEAD_DIM),
        token_position[:, :, None],
    ).astype(jnp.bfloat16)
    current_values = value_heads_all.reshape(step_total, row_total, KEY_VALUE_HEADS, HEAD_DIM)
    grouped_queries = query_heads_all.reshape(
        step_total, row_total, KEY_VALUE_HEADS, group_width, HEAD_DIM
    )
    block_length = key_value_cache.shape[2]
    stored_keys = key_value_cache[0].reshape(row_total, block_length, KEY_VALUE_HEADS, HEAD_DIM)
    stored_values = key_value_cache[1].reshape(row_total, block_length, KEY_VALUE_HEADS, HEAD_DIM)
    scale_factor = HEAD_DIM ** (-0.5)
    places = tensor_rank * block_length + jnp.arange(block_length, dtype=jnp.int32)
    valid_pos = (places[None, :] < lengths[:, None])[None, :, None, None, :]
    attention_scores = (
        jnp.einsum(
            "srjgd,rpjd->srjgp", grouped_queries, stored_keys, preferred_element_type=jnp.float32
        )
        * scale_factor
    )
    block_max = jnp.max(jnp.where(valid_pos, attention_scores, MASKED_SCORE), -1)
    weights = jnp.where(valid_pos, jnp.exp(attention_scores - block_max[..., None]), 0.0)
    totals = jnp.sum(weights, -1)
    numer_block = jnp.einsum(
        "srjgp,rpjd->srjgd",
        weights.astype(jnp.bfloat16),
        stored_values,
        preferred_element_type=jnp.float32,
    )
    block_max = block_max.reshape(step_total, row_total, QUERY_HEADS)
    totals = totals.reshape(step_total, row_total, QUERY_HEADS)
    numer_block = numer_block.reshape(step_total, row_total, QUERY_HEADS, HEAD_DIM)
    first_head = tensor_rank * local_heads
    full_max, full_total, full_numer = joined(
        (block_max, totals, numer_block), "tensor", combine_pair
    )
    cache_max = lax.dynamic_slice_in_dim(full_max, first_head, local_heads, 2)
    cache_total = lax.dynamic_slice_in_dim(full_total, first_head, local_heads, 2)
    cache_numer = lax.dynamic_slice_in_dim(full_numer, first_head, local_heads, 2)
    own_keys = lax.dynamic_slice_in_dim(
        jnp.repeat(current_keys, group_width, axis=2), first_head, local_heads, 2
    )
    own_values = lax.dynamic_slice_in_dim(
        jnp.repeat(current_values, group_width, axis=2), first_head, local_heads, 2
    )
    fresh = (
        jnp.einsum("srhd,trhd->srht", own_query, own_keys, preferred_element_type=jnp.float32)
        * scale_factor
    )
    causal = (jnp.arange(step_total)[:, None] >= jnp.arange(step_total)[None, :])[:, None, None, :]
    overall = jnp.maximum(cache_max, jnp.max(jnp.where(causal, fresh, MASKED_SCORE), -1))
    cache_weight = jnp.exp(cache_max - overall)
    fresh_weight = jnp.where(causal, jnp.exp(fresh - overall[..., None]), 0.0)
    denominator = cache_total * cache_weight + jnp.sum(fresh_weight, -1)
    numerator = cache_numer * cache_weight[..., None] + jnp.einsum(
        "srht,trhd->srhd", fresh_weight, own_values.astype(jnp.float32)
    )
    attention_result = (
        (numerator / denominator[..., None])
        .astype(jnp.bfloat16)
        .reshape(step_total * row_total, local_cols)
    )
    partial_out = jnp.dot(attention_result, output_weight, preferred_element_type=jnp.float32)
    attended = lax.psum(partial_out, "tensor").astype(jnp.bfloat16)
    return (attended.reshape(step_total, row_total, model_width), merged_query_weight, kv_merged)


def gather_kernel(
    hidden_hbm, gain_ref, down_ref, upq_ref, upkv_ref, wq_hbm, wkv_hbm, cache_hbm,
    pall_ref, uq_ref, uk_ref, uv_ref, nb_ref, wq_out, wkv_out, cache_out,
    pk, upq_g, upkv_g, hidden_ref, up_send, up_recv, b_send, b_recv, own_sem, load_sem,
):
    f32, bf16 = jnp.float32, jnp.bfloat16
    L, T = 4, 4
    l, t = lax.axis_index("learner"), lax.axis_index("tensor")
    tp = [lax.rem(t + d, T) for d in range(T)]
    lp = [lax.rem(l + d, L) for d in range(L)]
    barrier = pltpu.get_barrier_semaphore()
    for d in range(1, 4):
        pl.semaphore_signal(barrier, inc=1, device_id={"tensor": tp[d]}, device_id_type=MESH)
        pl.semaphore_signal(barrier, inc=1, device_id={"learner": lp[d]}, device_id_type=MESH)
    hload = pltpu.make_async_copy(hidden_hbm, hidden_ref, load_sem.at[0])
    hload.start()
    locals_ = [
        pltpu.make_async_copy(upq_ref, upq_g.at[l], load_sem.at[1]),
        pltpu.make_async_copy(upkv_ref, upkv_g.at[l], load_sem.at[2]),
    ]
    for k, (src, dst) in enumerate(
        ((wq_hbm, wq_out), (wkv_hbm, wkv_out), (cache_hbm, cache_out))
    ):
        locals_.append(pltpu.make_async_copy(src, dst, load_sem.at[3 + k]))
    shard = down_ref[...]
    rows = shard.shape[0]
    half = rows // 2
    pk[0:rows, :] = shard[:, :128]
    pk[rows : rows + half, :] = jnp.concatenate([shard[:half, 128:], shard[half:, 128:]], axis=1)
    pl.semaphore_wait(barrier, 6)

    waits = []
    l2 = lax.rem(l + 2, L)
    l1 = l + 1 - 2 * lax.rem(l, 2)
    l3 = lax.rem(l1 + 2, L)
    t1 = t + 1 - 2 * lax.rem(t, 2)
    zp = [t, t1, lax.rem(t + 2, T), lax.rem(t1 + 2, T)]

    def bulk(src, blk, dev):
        c = pltpu.make_async_remote_copy(
            src_ref=src, dst_ref=pall_ref.at[blk], send_sem=b_send.at[len(waits)], recv_sem=b_recv.at[blk],
            device_id=dev, device_id_type=MESH,
        )
        c.start()
        waits.append(c)

    def arrived(blk):
        pltpu.make_async_remote_copy(
            src_ref=pk, dst_ref=pall_ref.at[blk], send_sem=b_send.at[0], recv_sem=b_recv.at[blk],
            device_id={"tensor": t1}, device_id_type=MESH,
        ).wait_recv()

    b = l * T + t
    bulk(pk, b, {"learner": l2})
    for k in (1, 2, 3):
        bulk(pk, b, {"tensor": zp[k]})
    bulk(pk, b, {"learner": l1})
    own = pltpu.make_async_copy(pk, pall_ref.at[b], own_sem)
    own.start()
    ups = []
    for d in range(1, 4):
        for k, (src, dst) in enumerate(((upq_ref, upq_g), (upkv_ref, upkv_g))):
            c = pltpu.make_async_remote_copy(
                src_ref=src, dst_ref=dst.at[l], send_sem=up_send.at[k, d], recv_sem=up_recv.at[k, d],
                device_id={"learner": lp[d]}, device_id_type=MESH,
            )
            c.start()
            ups.append(c)
    for c in locals_:
        c.start()

    model = gain_ref.shape[1]
    hload.wait()
    wide = hidden_ref[...].astype(f32).reshape(16, model)
    inv = lax.rsqrt(jnp.mean(wide * wide, -1, keepdims=True) + NORM_EPSILON)
    normed = (wide * inv * gain_ref[...].astype(f32)).astype(bf16)
    wid = nb_ref.shape[2]
    for k in range(nb_ref.shape[0]):
        nb_ref[k] = normed[:, k * wid : (k + 1) * wid]
    uq_ref[...] = jnp.zeros_like(uq_ref)
    uk_ref[...] = jnp.zeros_like(uk_ref)
    uv_ref[...] = jnp.zeros_like(uv_ref)

    for k in (1, 2, 3):
        blk = l * T + zp[k]
        arrived(blk)
        bulk(pall_ref.at[blk], blk, {"learner": l2})
        bulk(pall_ref.at[blk], blk, {"learner": l1})
        blk = l2 * T + zp[k - 1]
        arrived(blk)
        bulk(pall_ref.at[blk], blk, {"learner": l1})
    for c in ups:
        c.wait_recv()
    for c in locals_[:2]:
        c.wait()
    uq_ref[0:64, :] = upq_g[...].reshape(64, upq_g.shape[2])
    kvg = upkv_g[...]
    uk_ref[64:128, :] = kvg[:, 0].reshape(64, upkv_g.shape[3])
    uv_ref[64:128, :] = kvg[:, 1].reshape(64, upkv_g.shape[3])
    blk = l2 * T + zp[3]
    arrived(blk)
    bulk(pall_ref.at[blk], blk, {"learner": l1})
    for k in range(4):
        arrived(l1 * T + k)
        arrived(l3 * T + k)
    own.wait()
    for c in locals_[2:]:
        c.wait()
    for c in ups + waits:
        c.wait_send()


def merge_kernel(
    p_ref, uq_ref, uk_ref, uv_ref, n_ref, wq_ref, wkv_ref, oq_ref, okv_ref, qs_ref, ks_ref, vs_ref
):
    f32, bf16 = jnp.float32, jnp.bfloat16
    rows = p_ref.shape[1] * 2 // 3
    half = rows // 2

    @pl.when(pl.program_id(0) == 0)
    def _():
        qs_ref[...] = jnp.zeros_like(qs_ref)
        ks_ref[...] = jnp.zeros_like(ks_ref)
        vs_ref[...] = jnp.zeros_like(vs_ref)

    uv_high = uv_ref[...]
    uv_low = jnp.concatenate([uv_high[64:], uv_high[:64]], axis=0)
    for e in range(p_ref.shape[0]):
        p = p_ref[e]
        qk, pv = p[:rows], p[rows:]
        cut = slice(e * rows, (e + 1) * rows)
        dq = jnp.dot(qk, uq_ref[...], preferred_element_type=f32)
        oq_ref[cut] = (wq_ref[cut].astype(f32) + ADAPTER_SCALE * dq).astype(bf16)
        dk = jnp.dot(qk, uk_ref[...], preferred_element_type=f32)
        okv_ref[0, cut] = (wkv_ref[0, cut].astype(f32) + ADAPTER_SCALE * dk).astype(bf16)
        for k, up in enumerate((uv_low, uv_high)):
            dv = jnp.dot(pv, up, preferred_element_type=f32)
            cut = slice(e * rows + k * half, e * rows + (k + 1) * half)
            okv_ref[1, cut] = (wkv_ref[1, cut].astype(f32) + ADAPTER_SCALE * dv).astype(bf16)
    n = n_ref[0]
    qs_ref[...] += jnp.dot(n, oq_ref[...], preferred_element_type=f32)
    ks_ref[...] += jnp.dot(n, okv_ref[0], preferred_element_type=f32)
    vs_ref[...] += jnp.dot(n, okv_ref[1], preferred_element_type=f32)


def decode_kernel(
    lengths_ref, qs_ref, ks_ref, vs_ref, cache, wo,
    att_ref,
    qtmp, qall, keyf, valf, nsend, nrecv, msend, mrecv, res, abuf,
    psend, precv, asend, arecv,
    q_send, q_recv, n_send, n_recv, m_send, m_recv, p_send, p_recv, a_send, a_recv,
):
    f32, bf16 = jnp.float32, jnp.bfloat16
    T = 4
    t = lax.axis_index("tensor")
    model = wo.shape[1]
    scale = HEAD_DIM ** (-0.5)
    tp = [lax.rem(t + d, T) for d in range(T)]

    def to_t(d):
        return {"tensor": tp[d]}

    barrier = pltpu.get_barrier_semaphore()
    for d in range(1, 4):
        pl.semaphore_signal(barrier, inc=1, device_id=to_t(d), device_id_type=MESH)
    waits = []

    def send(src, dst, ssem, rsem, dev):
        c = pltpu.make_async_remote_copy(
            src_ref=src, dst_ref=dst, send_sem=ssem, recv_sem=rsem, device_id=dev, device_id_type=MESH
        )
        c.start()
        waits.append(c)
        return c

    sub = lax.broadcasted_iota(jnp.int32, (16, 128), 0)
    lane = lax.broadcasted_iota(jnp.int32, (16, 128), 1)
    row = lax.rem(sub, 8)
    pos = jnp.zeros((16, 128), jnp.int32)
    for r in range(8):
        pos = jnp.where(row == r, lengths_ref[r], pos)
    pos = (pos + jnp.where(sub >= 8, 1, 0)).astype(f32)
    freq = jnp.exp(lax.rem(lane, 64).astype(f32) * (-2.0 / HEAD_DIM * math.log(ROPE_BASE)))
    cosine = jnp.cos(pos * freq)
    sine = jnp.sin(pos * freq)
    sine = jnp.where(lane < 64, -sine, sine)

    def rope(v):
        return v * cosine + pltpu.roll(v, 64, 1) * sine

    qacc = qs_ref[...]
    kacc = ks_ref[...].astype(bf16).astype(f32)
    valf[...] = vs_ref[...].astype(bf16).astype(f32)
    pl.semaphore_wait(barrier, 3)

    for h in range(8):
        v = rope(qacc[:, h * 128 : (h + 1) * 128])
        for s in range(2):
            start = (h // 4) * 8 + s * 4 + h % 4
            qtmp[pl.ds(start, 8, stride=16), :] = v[s * 8 : (s + 1) * 8, :]
    qall[0] = qtmp[...].astype(bf16)
    qs = [send(qall.at[0], qall.at[d], q_send.at[d], q_recv.at[d], to_t(d)) for d in range(1, 4)]
    for h in range(2):
        keyf[:, h * 128 : (h + 1) * 128] = rope(kacc[:, h * 128 : (h + 1) * 128]).astype(bf16).astype(f32)

    first = sub[:, 0:1] < 8
    place = t * cache.shape[2] + lax.broadcasted_iota(jnp.int32, (16, cache.shape[2]), 1)
    lane2 = lane
    ns_copies = [None] * 4
    per = 4

    def attend(d):
        owner = lax.rem(t + T - d, T)
        cols = pl.multiple_of(owner * 256, 256)

        def step(i, ml):
            for u in range(per):
                r = i * per + u
                q16 = qall[d, pl.ds(pl.multiple_of(r * 16, 16), 16), :]
                kk = cache[0, r, :, pl.ds(cols, 256)]
                vv = cache[1, r, :, pl.ds(cols, 256)]
                dims = (((1,), (1,)), ((), ()))
                s0 = lax.dot_general(q16, kk[:, :128], dims, preferred_element_type=f32)
                s1 = lax.dot_general(q16, kk[:, 128:], dims, preferred_element_type=f32)
                s = jnp.where(first, s0, s1) * scale
                valid = place < lengths_ref[r]
                m = jnp.max(jnp.where(valid, s, MASKED_SCORE), -1, keepdims=True)
                w = jnp.where(valid, jnp.exp(s - m), 0.0)
                tot = jnp.sum(w, -1, keepdims=True)
                nn = jnp.dot(w.astype(bf16), vv, preferred_element_type=f32)
                nn = jnp.where(first, nn[:, :128], nn[:, 128:])
                nsend[d, pl.ds(pl.multiple_of(r * 16, 16), 16), :] = nn.astype(nsend.dtype)
                ml = jnp.where(lane2 == r, m, jnp.where(lane2 == r + 8, tot, ml))
            return ml

        msend[d] = lax.fori_loop(0, 8 // per, step, jnp.zeros((16, 128), f32))

    attend(0)
    nsc, msc = [], []
    for d in range(1, 4):
        qs[d - 1].wait_recv()
        attend(d)
        back = 4 - d
        nsc.append(send(nsend.at[d], nrecv.at[back], n_send.at[d], n_recv.at[back], to_t(back)))
        msc.append(send(msend.at[d], mrecv.at[back], m_send.at[d], m_recv.at[back], to_t(back)))

    for c in nsc:
        c.wait_recv()
    for c in msc:
        c.wait_recv()
    nrecv[0] = nsend[0]
    mrecv[0] = msend[0]
    late = lax.rem(sub[:, 0:1] // 4, 2) == 1
    for r in range(8):
        q16 = qall[0, r * 16 : (r + 1) * 16, :].astype(f32)
        fresh = []
        vals = []
        for u in range(2):
            k16 = jnp.where(first, keyf[u * 8 + r : u * 8 + r + 1, 0:128], keyf[u * 8 + r : u * 8 + r + 1, 128:256])
            vals.append(
                jnp.where(first, valf[u * 8 + r : u * 8 + r + 1, 0:128], valf[u * 8 + r : u * 8 + r + 1, 128:256])
            )
            fresh.append(jnp.sum(q16 * k16, -1, keepdims=True) * scale)
        fresh[1] = jnp.where(late, fresh[1], MASKED_SCORE)
        ms = [mrecv[d, :, r : r + 1] for d in range(4)]
        top = jnp.maximum(fresh[0], fresh[1])
        for m in ms:
            top = jnp.maximum(top, m)
        w0 = jnp.exp(fresh[0] - top)
        w1 = jnp.where(late, jnp.exp(fresh[1] - top), 0.0)
        den = w0 + w1
        num = w0 * vals[0] + w1 * vals[1]
        for d in range(4):
            e = jnp.exp(ms[d] - top)
            den = den + e * mrecv[d, :, 8 + r : 9 + r]
            num = num + e * nrecv[d, r * 16 : (r + 1) * 16, :].astype(f32)
        res[r * 16 : (r + 1) * 16, :] = num / den
    for h in range(8):
        for s in range(2):
            start = (h // 4) * 8 + s * 4 + h % 4
            abuf[s * 8 : (s + 1) * 8, h * 128 : (h + 1) * 128] = res[pl.ds(start, 8, stride=16), :]
    a = abuf[...].astype(bf16)

    quarter = model // T
    ps = []
    for d in (2, 1, 3):
        o = jnp.dot(a, wo[:, pl.ds(pl.multiple_of(tp[d] * quarter, 128), quarter)], preferred_element_type=f32)
        psend[d] = o.astype(bf16)
        ps.append(send(psend.at[d], precv.at[d], p_send.at[d], p_recv.at[d], to_t(d)))
    total = jnp.dot(a, wo[:, pl.ds(pl.multiple_of(t * quarter, 128), quarter)], preferred_element_type=f32)

    for c in ps:
        c.wait_recv()
    for d in range(1, 4):
        total = total + precv[d].astype(f32)
    asend[...] = total.astype(bf16)
    acs = [send(asend, arecv.at[t], a_send.at[d], a_recv.at[d], to_t(d)) for d in range(1, 4)]
    arecv[t] = asend[...]
    for c in acs:
        c.wait_recv()
    for k in range(4):
        both = arecv[k].astype(f32)
        for s in range(2):
            att_ref[s, :, k * quarter : (k + 1) * quarter] = both[s * 8 : (s + 1) * 8, :].astype(bf16)
    for c in waits:
        c.wait_send()


def fused_device(
    hidden, input_norm_gain, lengths, key_value_cache, query_base_weight, key_value_weight,
    output_weight, adapter_down, query_up_factor, key_value_up,
):
    f32, bf16 = jnp.float32, jnp.bfloat16
    model = hidden.shape[2]
    part = model // 4
    rows = adapter_down.shape[0]
    packed = rows + rows // 2
    steps = 8
    V, A, S = pltpu.VMEM, pl.ANY, pltpu.SMEM
    dma = pltpu.SemaphoreType.DMA
    spec = lambda m: pl.BlockSpec(memory_space=m)
    shape = jax.ShapeDtypeStruct
    p_all, uq, uk, uv, blocks, wq_v, wkv_v, cache_v = pl.pallas_call(
        gather_kernel,
        out_shape=[
            shape((16, packed, 128), bf16), shape((128, 1024), bf16), shape((128, 256), bf16),
            shape((128, 256), bf16), shape((steps, 16, model // steps), bf16),
            shape(query_base_weight.shape, bf16), shape(key_value_weight.shape, bf16),
            shape(key_value_cache.shape, bf16),
        ],
        in_specs=[spec(A), spec(V), spec(V)] + [spec(A)] * 5,
        out_specs=[spec(A)] + [spec(V)] * 4 + [spec(A)] * 3,
        scratch_shapes=[
            V((packed, 128), bf16), V((4, 16, 1024), bf16), V((4, 2, 16, 256), bf16), V(hidden.shape, bf16),
            dma((2, 4)), dma((2, 4)), dma((15,)), dma((16,)), dma, dma((6,)),
        ],
        compiler_params=pltpu.CompilerParams(
            collective_id=0, has_side_effects=True, vmem_limit_bytes=6 * 1024 * 1024
        ),
        name="gather",
    )(hidden, input_norm_gain.reshape(1, model), adapter_down, query_up_factor, key_value_up,
      query_base_weight, key_value_weight, key_value_cache)
    wide = model // steps
    whole = lambda *sh: pl.BlockSpec(sh, lambda i: (0,) * len(sh))
    merged, kv_merged, qs, ks, vs = pl.pallas_call(
        merge_kernel,
        grid=(steps,),
        out_shape=[
            shape(query_base_weight.shape, bf16), shape(key_value_weight.shape, bf16),
            shape((16, 1024), f32), shape((16, 256), f32), shape((16, 256), f32),
        ],
        in_specs=[
            pl.BlockSpec((16 // steps, packed, 128), lambda i: (i, 0, 0)),
            whole(128, 1024), whole(128, 256), whole(128, 256),
            pl.BlockSpec((1, 16, wide), lambda i: (i, 0, 0)),
            pl.BlockSpec((wide, 1024), lambda i: (i, 0)),
            pl.BlockSpec((2, wide, 256), lambda i: (0, i, 0)),
        ],
        out_specs=[
            pl.BlockSpec((wide, 1024), lambda i: (i, 0)),
            pl.BlockSpec((2, wide, 256), lambda i: (0, i, 0)),
            whole(16, 1024), whole(16, 256), whole(16, 256),
        ],
        compiler_params=pltpu.CompilerParams(vmem_limit_bytes=14 * 1024 * 1024),
        name="merge",
    )(p_all, uq, uk, uv, blocks, wq_v, wkv_v)
    attended = pl.pallas_call(
        decode_kernel,
        out_shape=shape(hidden.shape, bf16),
        in_specs=[spec(S)] + [spec(V)] * 5,
        out_specs=spec(V),
        scratch_shapes=[
            V((128, 128), f32), V((4, 128, 128), bf16), V((16, 256), f32), V((16, 256), f32),
            V((4, 128, 128), bf16), V((4, 128, 128), bf16), V((4, 16, 128), f32), V((4, 16, 128), f32),
            V((128, 128), f32), V((16, 1024), f32),
            V((4, 16, part), bf16), V((4, 16, part), bf16), V((16, part), bf16), V((4, 16, part), bf16),
        ]
        + [dma((4,))] * 10,
        compiler_params=pltpu.CompilerParams(
            collective_id=1, has_side_effects=True, vmem_limit_bytes=10 * 1024 * 1024
        ),
        name="decode",
    )(lengths, qs, ks, vs, cache_v, output_weight)
    return attended, merged, kv_merged


def solution(mesh):
    small = mesh.shape["learner"] == 4 and mesh.shape["tensor"] == 4
    return jax.shard_map(
        fused_device if small else per_device,
        mesh=mesh,
        in_specs=(
            P(None, ("groups", "learner"), None),
            P(),
            P(("groups", "learner")),
            P(None, ("groups", "learner"), "tensor", None),
            P(None, "tensor"),
            P(None, None, "tensor"),
            P("tensor", None),
            P(("groups", "learner", "tensor"), None),
            P(("groups", "learner"), "tensor"),
            P(None, ("groups", "learner"), "tensor"),
        ),
        out_specs=(
            P(None, ("groups", "learner"), None),
            P("groups", "tensor"),
            P(None, "groups", "tensor"),
        ),
        check_vma=False,
    )
```

```python
import math
import jax
import jax.numpy as jnp
from jax import lax
from jax.experimental import pallas as pl
from jax.experimental.pallas import tpu as pltpu
from jax.sharding import PartitionSpec as P

QUERY_HEADS = 32
KEY_VALUE_HEADS = 8
HEAD_DIM = 128
MESH = pl.DeviceIdType.MESH


ADAPTER_SCALE = 2.0
ROPE_BASE = 1000000.0
MASKED_SCORE = -1e30
NORM_EPSILON = 1e-06


def joined(part, axis, combine):
    gathered = jax.tree.map(lambda a: lax.all_gather(a, axis), part)

    def take(source):
        return jax.tree.map(lambda a: lax.dynamic_index_in_dim(a, source, 0, False), gathered)

    return lax.fori_loop(
        1, lax.axis_size(axis), lambda source, state: combine(state, take(source)), take(0)
    )


def apply_rotary(values, token_position):
    half_dim = values.shape[-1] // 2
    inverse = ROPE_BASE ** (-jnp.arange(half_dim, dtype=jnp.float32) * 2.0 / values.shape[-1])
    angles = token_position[..., None] * inverse
    cosine = jnp.concatenate([jnp.cos(angles), jnp.cos(angles)], -1)
    sine_table = jnp.concatenate([jnp.sin(angles), jnp.sin(angles)], -1)
    turned = jnp.concatenate([-values[..., half_dim:], values[..., :half_dim]], -1)
    return values * cosine + turned * sine_table


def combine_pair(former, latter):
    highest = jnp.maximum(former[0], latter[0])
    former_scale = jnp.exp(former[0] - highest)
    latter_scale = jnp.exp(latter[0] - highest)
    return (
        highest,
        former[1] * former_scale + latter[1] * latter_scale,
        former[2] * former_scale[..., None] + latter[2] * latter_scale[..., None],
    )


def per_device(
    hidden,
    input_norm_gain,
    lengths,
    key_value_cache,
    query_base_weight,
    key_value_weight,
    output_weight,
    adapter_down,
    query_up_factor,
    key_value_up,
):
    step_total, row_total, model_width = hidden.shape
    group_width = QUERY_HEADS // KEY_VALUE_HEADS
    tensor_rank = lax.axis_index("tensor")
    local_cols = query_base_weight.shape[1]
    local_heads = local_cols // HEAD_DIM
    widened = hidden.astype(jnp.float32)
    normed = (
        widened
        * lax.rsqrt(jnp.mean(widened * widened, -1, keepdims=True) + NORM_EPSILON)
        * input_norm_gain.astype(jnp.float32)
    ).astype(jnp.bfloat16)
    flattened_rows = normed.reshape(step_total * row_total, model_width)
    query_delta, key_value_delta = (
        lax.all_gather(query_up_factor, "learner", axis=0, tiled=True),
        lax.all_gather(key_value_up, "learner", axis=1, tiled=True),
    )
    adapter_rank = query_delta.shape[0]
    down_slice = lax.all_gather(adapter_down, ("learner", "tensor"), axis=0, tiled=True)
    query_rows = (
        query_base_weight.astype(jnp.float32)
        + ADAPTER_SCALE
        * jnp.dot(down_slice[:, :adapter_rank], query_delta, preferred_element_type=jnp.float32)
    ).astype(jnp.bfloat16)
    key_rows = (
        key_value_weight[0].astype(jnp.float32)
        + ADAPTER_SCALE
        * jnp.dot(
            down_slice[:, adapter_rank : 2 * adapter_rank],
            key_value_delta[0],
            preferred_element_type=jnp.float32,
        )
    ).astype(jnp.bfloat16)
    value_row_list = (
        key_value_weight[1].astype(jnp.float32)
        + ADAPTER_SCALE
        * jnp.dot(
            down_slice[:, 2 * adapter_rank :],
            key_value_delta[1],
            preferred_element_type=jnp.float32,
        )
    ).astype(jnp.bfloat16)
    query_sum = jnp.dot(flattened_rows, query_rows, preferred_element_type=jnp.float32)
    key_sum = jnp.dot(flattened_rows, key_rows, preferred_element_type=jnp.float32)
    value_sum = jnp.dot(flattened_rows, value_row_list, preferred_element_type=jnp.float32)
    merged_query_weight = query_rows
    kv_merged = jnp.stack([key_rows, value_row_list])
    query_sum, key_sum, value_sum, merged_query_weight, kv_merged = (
        query_sum,
        key_sum,
        value_sum,
        merged_query_weight,
        kv_merged,
    )
    token_position = (lengths[None, :] + jnp.arange(step_total, dtype=jnp.int32)[:, None]).astype(
        jnp.float32
    )
    own_query = apply_rotary(
        query_sum.reshape(step_total, row_total, local_heads, HEAD_DIM), token_position[:, :, None]
    ).astype(jnp.bfloat16)
    query_heads_all, key_all, value_heads_all = (
        lax.all_gather(
            own_query.reshape(step_total * row_total, local_cols), "tensor", axis=1, tiled=True
        ),
        lax.all_gather(key_sum.astype(jnp.bfloat16), "tensor", axis=1, tiled=True),
        lax.all_gather(value_sum.astype(jnp.bfloat16), "tensor", axis=1, tiled=True),
    )
    current_keys = apply_rotary(
        lax.optimization_barrier(key_all)
        .astype(jnp.float32)
        .reshape(step_total, row_total, KEY_VALUE_HEADS, HEAD_DIM),
        token_position[:, :, None],
    ).astype(jnp.bfloat16)
    current_values = value_heads_all.reshape(step_total, row_total, KEY_VALUE_HEADS, HEAD_DIM)
    grouped_queries = query_heads_all.reshape(
        step_total, row_total, KEY_VALUE_HEADS, group_width, HEAD_DIM
    )
    block_length = key_value_cache.shape[2]
    stored_keys = key_value_cache[0].reshape(row_total, block_length, KEY_VALUE_HEADS, HEAD_DIM)
    stored_values = key_value_cache[1].reshape(row_total, block_length, KEY_VALUE_HEADS, HEAD_DIM)
    scale_factor = HEAD_DIM ** (-0.5)
    places = tensor_rank * block_length + jnp.arange(block_length, dtype=jnp.int32)
    valid_pos = (places[None, :] < lengths[:, None])[None, :, None, None, :]
    attention_scores = (
        jnp.einsum(
            "srjgd,rpjd->srjgp", grouped_queries, stored_keys, preferred_element_type=jnp.float32
        )
        * scale_factor
    )
    block_max = jnp.max(jnp.where(valid_pos, attention_scores, MASKED_SCORE), -1)
    weights = jnp.where(valid_pos, jnp.exp(attention_scores - block_max[..., None]), 0.0)
    totals = jnp.sum(weights, -1)
    numer_block = jnp.einsum(
        "srjgp,rpjd->srjgd",
        weights.astype(jnp.bfloat16),
        stored_values,
        preferred_element_type=jnp.float32,
    )
    block_max = block_max.reshape(step_total, row_total, QUERY_HEADS)
    totals = totals.reshape(step_total, row_total, QUERY_HEADS)
    numer_block = numer_block.reshape(step_total, row_total, QUERY_HEADS, HEAD_DIM)
    first_head = tensor_rank * local_heads
    full_max, full_total, full_numer = joined(
        (block_max, totals, numer_block), "tensor", combine_pair
    )
    cache_max = lax.dynamic_slice_in_dim(full_max, first_head, local_heads, 2)
    cache_total = lax.dynamic_slice_in_dim(full_total, first_head, local_heads, 2)
    cache_numer = lax.dynamic_slice_in_dim(full_numer, first_head, local_heads, 2)
    own_keys = lax.dynamic_slice_in_dim(
        jnp.repeat(current_keys, group_width, axis=2), first_head, local_heads, 2
    )
    own_values = lax.dynamic_slice_in_dim(
        jnp.repeat(current_values, group_width, axis=2), first_head, local_heads, 2
    )
    fresh = (
        jnp.einsum("srhd,trhd->srht", own_query, own_keys, preferred_element_type=jnp.float32)
        * scale_factor
    )
    causal = (jnp.arange(step_total)[:, None] >= jnp.arange(step_total)[None, :])[:, None, None, :]
    overall = jnp.maximum(cache_max, jnp.max(jnp.where(causal, fresh, MASKED_SCORE), -1))
    cache_weight = jnp.exp(cache_max - overall)
    fresh_weight = jnp.where(causal, jnp.exp(fresh - overall[..., None]), 0.0)
    denominator = cache_total * cache_weight + jnp.sum(fresh_weight, -1)
    numerator = cache_numer * cache_weight[..., None] + jnp.einsum(
        "srht,trhd->srhd", fresh_weight, own_values.astype(jnp.float32)
    )
    attention_result = (
        (numerator / denominator[..., None])
        .astype(jnp.bfloat16)
        .reshape(step_total * row_total, local_cols)
    )
    partial_out = jnp.dot(attention_result, output_weight, preferred_element_type=jnp.float32)
    attended = lax.psum(partial_out, "tensor").astype(jnp.bfloat16)
    return (attended.reshape(step_total, row_total, model_width), merged_query_weight, kv_merged)


def gather_kernel(
    hidden_hbm, gain_ref, down_ref, upq_ref, upkv_ref, wq_hbm, wkv_hbm, cache_hbm,
    pall_ref, uq_ref, uk_ref, uv_ref, nb_ref, wq_out, wkv_out, cache_out,
    pk, upq_g, upkv_g, hidden_ref, up_send, up_recv, b_send, b_recv, own_sem, load_sem,
):
    f32, bf16 = jnp.float32, jnp.bfloat16
    L, T = 4, 4
    l, t = lax.axis_index("learner"), lax.axis_index("tensor")
    tp = [lax.rem(t + d, T) for d in range(T)]
    lp = [lax.rem(l + d, L) for d in range(L)]
    barrier = pltpu.get_barrier_semaphore()
    for d in range(1, 4):
        pl.semaphore_signal(barrier, inc=1, device_id={"tensor": tp[d]}, device_id_type=MESH)
        pl.semaphore_signal(barrier, inc=1, device_id={"learner": lp[d]}, device_id_type=MESH)
    hload = pltpu.make_async_copy(hidden_hbm, hidden_ref, load_sem.at[0])
    hload.start()
    locals_ = [
        pltpu.make_async_copy(upq_ref, upq_g.at[l], load_sem.at[1]),
        pltpu.make_async_copy(upkv_ref, upkv_g.at[l], load_sem.at[2]),
    ]
    for k, (src, dst) in enumerate(
        ((wq_hbm, wq_out), (wkv_hbm, wkv_out), (cache_hbm, cache_out))
    ):
        locals_.append(pltpu.make_async_copy(src, dst, load_sem.at[3 + k]))
    shard = down_ref[...]
    rows = shard.shape[0]
    half = rows // 2
    pk[0:rows, :] = shard[:, :128]
    pk[rows : rows + half, :] = jnp.concatenate([shard[:half, 128:], shard[half:, 128:]], axis=1)
    pl.semaphore_wait(barrier, 6)

    waits = []
    l2 = lax.rem(l + 2, L)
    l1 = l + 1 - 2 * lax.rem(l, 2)
    l3 = lax.rem(l1 + 2, L)
    t1 = t + 1 - 2 * lax.rem(t, 2)
    zp = [t, t1, lax.rem(t + 2, T), lax.rem(t1 + 2, T)]

    def bulk(src, blk, dev):
        c = pltpu.make_async_remote_copy(
            src_ref=src, dst_ref=pall_ref.at[blk], send_sem=b_send.at[len(waits)], recv_sem=b_recv.at[blk],
            device_id=dev, device_id_type=MESH,
        )
        c.start()
        waits.append(c)

    def arrived(blk):
        pltpu.make_async_remote_copy(
            src_ref=pk, dst_ref=pall_ref.at[blk], send_sem=b_send.at[0], recv_sem=b_recv.at[blk],
            device_id={"tensor": t1}, device_id_type=MESH,
        ).wait_recv()

    b = l * T + t
    bulk(pk, b, {"learner": l2})
    for k in (1, 2, 3):
        bulk(pk, b, {"tensor": zp[k]})
    bulk(pk, b, {"learner": l1})
    own = pltpu.make_async_copy(pk, pall_ref.at[b], own_sem)
    own.start()
    ups = []
    for d in range(1, 4):
        for k, (src, dst) in enumerate(((upq_ref, upq_g), (upkv_ref, upkv_g))):
            c = pltpu.make_async_remote_copy(
                src_ref=src, dst_ref=dst.at[l], send_sem=up_send.at[k, d], recv_sem=up_recv.at[k, d],
                device_id={"learner": lp[d]}, device_id_type=MESH,
            )
            c.start()
            ups.append(c)
    for c in locals_:
        c.start()

    model = gain_ref.shape[1]
    hload.wait()
    wide = hidden_ref[...].astype(f32).reshape(16, model)
    inv = lax.rsqrt(jnp.mean(wide * wide, -1, keepdims=True) + NORM_EPSILON)
    normed = (wide * inv * gain_ref[...].astype(f32)).astype(bf16)
    wid = nb_ref.shape[2]
    for k in range(nb_ref.shape[0]):
        nb_ref[k] = normed[:, k * wid : (k + 1) * wid]
    uq_ref[...] = jnp.zeros_like(uq_ref)
    uk_ref[...] = jnp.zeros_like(uk_ref)
    uv_ref[...] = jnp.zeros_like(uv_ref)

    for k in (1, 2, 3):
        blk = l * T + zp[k]
        arrived(blk)
        bulk(pall_ref.at[blk], blk, {"learner": l2})
        bulk(pall_ref.at[blk], blk, {"learner": l1})
        blk = l2 * T + zp[k - 1]
        arrived(blk)
        bulk(pall_ref.at[blk], blk, {"learner": l1})
    for c in ups:
        c.wait_recv()
    for c in locals_[:2]:
        c.wait()
    uq_ref[0:64, :] = upq_g[...].reshape(64, upq_g.shape[2])
    kvg = upkv_g[...]
    uk_ref[64:128, :] = kvg[:, 0].reshape(64, upkv_g.shape[3])
    uv_ref[64:128, :] = kvg[:, 1].reshape(64, upkv_g.shape[3])
    blk = l2 * T + zp[3]
    arrived(blk)
    bulk(pall_ref.at[blk], blk, {"learner": l1})
    for k in range(4):
        arrived(l1 * T + k)
        arrived(l3 * T + k)
    own.wait()
    for c in locals_[2:]:
        c.wait()
    for c in ups + waits:
        c.wait_send()


def merge_kernel(
    p_ref, uq_ref, uk_ref, uv_ref, n_ref, wq_ref, wkv_ref, oq_ref, okv_ref, qs_ref, ks_ref, vs_ref
):
    f32, bf16 = jnp.float32, jnp.bfloat16
    rows = p_ref.shape[1] * 2 // 3
    half = rows // 2

    @pl.when(pl.program_id(0) == 0)
    def _():
        qs_ref[...] = jnp.zeros_like(qs_ref)
        ks_ref[...] = jnp.zeros_like(ks_ref)
        vs_ref[...] = jnp.zeros_like(vs_ref)

    uv_high = uv_ref[...]
    uv_low = jnp.concatenate([uv_high[64:], uv_high[:64]], axis=0)
    for e in range(p_ref.shape[0]):
        p = p_ref[e]
        qk, pv = p[:rows], p[rows:]
        cut = slice(e * rows, (e + 1) * rows)
        dq = jnp.dot(qk, uq_ref[...], preferred_element_type=f32)
        oq_ref[cut] = (wq_ref[cut].astype(f32) + ADAPTER_SCALE * dq).astype(bf16)
        dk = jnp.dot(qk, uk_ref[...], preferred_element_type=f32)
        okv_ref[0, cut] = (wkv_ref[0, cut].astype(f32) + ADAPTER_SCALE * dk).astype(bf16)
        for k, up in enumerate((uv_low, uv_high)):
            dv = jnp.dot(pv, up, preferred_element_type=f32)
            cut = slice(e * rows + k * half, e * rows + (k + 1) * half)
            okv_ref[1, cut] = (wkv_ref[1, cut].astype(f32) + ADAPTER_SCALE * dv).astype(bf16)
    n = n_ref[0]
    qs_ref[...] += jnp.dot(n, oq_ref[...], preferred_element_type=f32)
    ks_ref[...] += jnp.dot(n, okv_ref[0], preferred_element_type=f32)
    vs_ref[...] += jnp.dot(n, okv_ref[1], preferred_element_type=f32)


def decode_kernel(
    lengths_ref, qs_ref, ks_ref, vs_ref, cache, wo,
    att_ref,
    qtmp, qall, keyf, valf, nsend, nrecv, msend, mrecv, res, abuf,
    psend, precv, asend, arecv,
    q_send, q_recv, n_send, n_recv, m_send, m_recv, p_send, p_recv, a_send, a_recv,
):
    f32, bf16 = jnp.float32, jnp.bfloat16
    T = 4
    t = lax.axis_index("tensor")
    model = wo.shape[1]
    scale = HEAD_DIM ** (-0.5)
    tp = [lax.rem(t + d, T) for d in range(T)]

    def to_t(d):
        return {"tensor": tp[d]}

    barrier = pltpu.get_barrier_semaphore()
    for d in range(1, 4):
        pl.semaphore_signal(barrier, inc=1, device_id=to_t(d), device_id_type=MESH)
    waits = []

    def send(src, dst, ssem, rsem, dev):
        c = pltpu.make_async_remote_copy(
            src_ref=src, dst_ref=dst, send_sem=ssem, recv_sem=rsem, device_id=dev, device_id_type=MESH
        )
        c.start()
        waits.append(c)
        return c

    sub = lax.broadcasted_iota(jnp.int32, (16, 128), 0)
    lane = lax.broadcasted_iota(jnp.int32, (16, 128), 1)
    row = lax.rem(sub, 8)
    pos = jnp.zeros((16, 128), jnp.int32)
    for r in range(8):
        pos = jnp.where(row == r, lengths_ref[r], pos)
    pos = (pos + jnp.where(sub >= 8, 1, 0)).astype(f32)
    freq = jnp.exp(lax.rem(lane, 64).astype(f32) * (-2.0 / HEAD_DIM * math.log(ROPE_BASE)))
    cosine = jnp.cos(pos * freq)
    sine = jnp.sin(pos * freq)
    sine = jnp.where(lane < 64, -sine, sine)

    def rope(v):
        return v * cosine + pltpu.roll(v, 64, 1) * sine

    qacc = qs_ref[...]
    kacc = ks_ref[...].astype(bf16).astype(f32)
    valf[...] = vs_ref[...].astype(bf16).astype(f32)
    pl.semaphore_wait(barrier, 3)

    for h in range(8):
        v = rope(qacc[:, h * 128 : (h + 1) * 128])
        for s in range(2):
            start = (h // 4) * 8 + s * 4 + h % 4
            qtmp[pl.ds(start, 8, stride=16), :] = v[s * 8 : (s + 1) * 8, :]
    qall[0] = qtmp[...].astype(bf16)
    qs = [send(qall.at[0], qall.at[d], q_send.at[d], q_recv.at[d], to_t(d)) for d in range(1, 4)]
    for h in range(2):
        keyf[:, h * 128 : (h + 1) * 128] = rope(kacc[:, h * 128 : (h + 1) * 128]).astype(bf16).astype(f32)

    first = sub[:, 0:1] < 8
    place = t * cache.shape[2] + lax.broadcasted_iota(jnp.int32, (16, cache.shape[2]), 1)
    lane2 = lane
    ns_copies = [None] * 4
    per = 8

    def attend(d):
        owner = lax.rem(t + T - d, T)
        cols = pl.multiple_of(owner * 256, 256)

        def step(i, ml):
            for u in range(per):
                r = i * per + u
                q16 = qall[d, pl.ds(pl.multiple_of(r * 16, 16), 16), :]
                kk = cache[0, r, :, pl.ds(cols, 256)]
                vv = cache[1, r, :, pl.ds(cols, 256)]
                dims = (((1,), (1,)), ((), ()))
                s0 = lax.dot_general(q16, kk[:, :128], dims, preferred_element_type=f32)
                s1 = lax.dot_general(q16, kk[:, 128:], dims, preferred_element_type=f32)
                s = jnp.where(first, s0, s1) * scale
                valid = place < lengths_ref[r]
                m = jnp.max(jnp.where(valid, s, MASKED_SCORE), -1, keepdims=True)
                w = jnp.where(valid, jnp.exp(s - m), 0.0)
                tot = jnp.sum(w, -1, keepdims=True)
                nn = jnp.dot(w.astype(bf16), vv, preferred_element_type=f32)
                nn = jnp.where(first, nn[:, :128], nn[:, 128:])
                nsend[d, pl.ds(pl.multiple_of(r * 16, 16), 16), :] = nn.astype(nsend.dtype)
                ml = jnp.where(lane2 == r, m, jnp.where(lane2 == r + 8, tot, ml))
            return ml

        msend[d] = lax.fori_loop(0, 8 // per, step, jnp.zeros((16, 128), f32))

    attend(0)
    nsc, msc = [], []
    for d in range(1, 4):
        qs[d - 1].wait_recv()
        attend(d)
        back = 4 - d
        nsc.append(send(nsend.at[d], nrecv.at[back], n_send.at[d], n_recv.at[back], to_t(back)))
        msc.append(send(msend.at[d], mrecv.at[back], m_send.at[d], m_recv.at[back], to_t(back)))

    for c in nsc:
        c.wait_recv()
    for c in msc:
        c.wait_recv()
    nrecv[0] = nsend[0]
    mrecv[0] = msend[0]
    late = lax.rem(sub[:, 0:1] // 4, 2) == 1
    for r in range(8):
        q16 = qall[0, r * 16 : (r + 1) * 16, :].astype(f32)
        fresh = []
        vals = []
        for u in range(2):
            k16 = jnp.where(first, keyf[u * 8 + r : u * 8 + r + 1, 0:128], keyf[u * 8 + r : u * 8 + r + 1, 128:256])
            vals.append(
                jnp.where(first, valf[u * 8 + r : u * 8 + r + 1, 0:128], valf[u * 8 + r : u * 8 + r + 1, 128:256])
            )
            fresh.append(jnp.sum(q16 * k16, -1, keepdims=True) * scale)
        fresh[1] = jnp.where(late, fresh[1], MASKED_SCORE)
        ms = [mrecv[d, :, r : r + 1] for d in range(4)]
        top = jnp.maximum(fresh[0], fresh[1])
        for m in ms:
            top = jnp.maximum(top, m)
        w0 = jnp.exp(fresh[0] - top)
        w1 = jnp.where(late, jnp.exp(fresh[1] - top), 0.0)
        den = w0 + w1
        num = w0 * vals[0] + w1 * vals[1]
        for d in range(4):
            e = jnp.exp(ms[d] - top)
            den = den + e * mrecv[d, :, 8 + r : 9 + r]
            num = num + e * nrecv[d, r * 16 : (r + 1) * 16, :].astype(f32)
        res[r * 16 : (r + 1) * 16, :] = num / den
    for h in range(8):
        for s in range(2):
            start = (h // 4) * 8 + s * 4 + h % 4
            abuf[s * 8 : (s + 1) * 8, h * 128 : (h + 1) * 128] = res[pl.ds(start, 8, stride=16), :]
    a = abuf[...].astype(bf16)

    quarter = model // T
    ps = []
    for d in (2, 1, 3):
        o = jnp.dot(a, wo[:, pl.ds(pl.multiple_of(tp[d] * quarter, 128), quarter)], preferred_element_type=f32)
        psend[d] = o.astype(bf16)
        ps.append(send(psend.at[d], precv.at[d], p_send.at[d], p_recv.at[d], to_t(d)))
    total = jnp.dot(a, wo[:, pl.ds(pl.multiple_of(t * quarter, 128), quarter)], preferred_element_type=f32)

    for c in ps:
        c.wait_recv()
    for d in range(1, 4):
        total = total + precv[d].astype(f32)
    asend[...] = total.astype(bf16)
    acs = [send(asend, arecv.at[t], a_send.at[d], a_recv.at[d], to_t(d)) for d in range(1, 4)]
    arecv[t] = asend[...]
    for c in acs:
        c.wait_recv()
    for k in range(4):
        both = arecv[k].astype(f32)
        for s in range(2):
            att_ref[s, :, k * quarter : (k + 1) * quarter] = both[s * 8 : (s + 1) * 8, :].astype(bf16)
    for c in waits:
        c.wait_send()


def fused_device(
    hidden, input_norm_gain, lengths, key_value_cache, query_base_weight, key_value_weight,
    output_weight, adapter_down, query_up_factor, key_value_up,
):
    f32, bf16 = jnp.float32, jnp.bfloat16
    model = hidden.shape[2]
    part = model // 4
    rows = adapter_down.shape[0]
    packed = rows + rows // 2
    steps = 8
    V, A, S = pltpu.VMEM, pl.ANY, pltpu.SMEM
    dma = pltpu.SemaphoreType.DMA
    spec = lambda m: pl.BlockSpec(memory_space=m)
    shape = jax.ShapeDtypeStruct
    p_all, uq, uk, uv, blocks, wq_v, wkv_v, cache_v = pl.pallas_call(
        gather_kernel,
        out_shape=[
            shape((16, packed, 128), bf16), shape((128, 1024), bf16), shape((128, 256), bf16),
            shape((128, 256), bf16), shape((steps, 16, model // steps), bf16),
            shape(query_base_weight.shape, bf16), shape(key_value_weight.shape, bf16),
            shape(key_value_cache.shape, bf16),
        ],
        in_specs=[spec(A), spec(V), spec(V)] + [spec(A)] * 5,
        out_specs=[spec(A)] + [spec(V)] * 4 + [spec(A)] * 3,
        scratch_shapes=[
            V((packed, 128), bf16), V((4, 16, 1024), bf16), V((4, 2, 16, 256), bf16), V(hidden.shape, bf16),
            dma((2, 4)), dma((2, 4)), dma((15,)), dma((16,)), dma, dma((6,)),
        ],
        compiler_params=pltpu.CompilerParams(
            collective_id=0, has_side_effects=True, vmem_limit_bytes=6 * 1024 * 1024
        ),
        name="gather",
    )(hidden, input_norm_gain.reshape(1, model), adapter_down, query_up_factor, key_value_up,
      query_base_weight, key_value_weight, key_value_cache)
    wide = model // steps
    whole = lambda *sh: pl.BlockSpec(sh, lambda i: (0,) * len(sh))
    merged, kv_merged, qs, ks, vs = pl.pallas_call(
        merge_kernel,
        grid=(steps,),
        out_shape=[
            shape(query_base_weight.shape, bf16), shape(key_value_weight.shape, bf16),
            shape((16, 1024), f32), shape((16, 256), f32), shape((16, 256), f32),
        ],
        in_specs=[
            pl.BlockSpec((16 // steps, packed, 128), lambda i: (i, 0, 0)),
            whole(128, 1024), whole(128, 256), whole(128, 256),
            pl.BlockSpec((1, 16, wide), lambda i: (i, 0, 0)),
            pl.BlockSpec((wide, 1024), lambda i: (i, 0)),
            pl.BlockSpec((2, wide, 256), lambda i: (0, i, 0)),
        ],
        out_specs=[
            pl.BlockSpec((wide, 1024), lambda i: (i, 0)),
            pl.BlockSpec((2, wide, 256), lambda i: (0, i, 0)),
            whole(16, 1024), whole(16, 256), whole(16, 256),
        ],
        compiler_params=pltpu.CompilerParams(vmem_limit_bytes=14 * 1024 * 1024),
        name="merge",
    )(p_all, uq, uk, uv, blocks, wq_v, wkv_v)
    attended = pl.pallas_call(
        decode_kernel,
        out_shape=shape(hidden.shape, bf16),
        in_specs=[spec(S)] + [spec(V)] * 5,
        out_specs=spec(V),
        scratch_shapes=[
            V((128, 128), f32), V((4, 128, 128), bf16), V((16, 256), f32), V((16, 256), f32),
            V((4, 128, 128), bf16), V((4, 128, 128), bf16), V((4, 16, 128), f32), V((4, 16, 128), f32),
            V((128, 128), f32), V((16, 1024), f32),
            V((4, 16, part), bf16), V((4, 16, part), bf16), V((16, part), bf16), V((4, 16, part), bf16),
        ]
        + [dma((4,))] * 10,
        compiler_params=pltpu.CompilerParams(
            collective_id=1, has_side_effects=True, vmem_limit_bytes=10 * 1024 * 1024
        ),
        name="decode",
    )(lengths, qs, ks, vs, cache_v, output_weight)
    return attended, merged, kv_merged


def solution(mesh):
    small = mesh.shape["learner"] == 4 and mesh.shape["tensor"] == 4
    return jax.shard_map(
        fused_device if small else per_device,
        mesh=mesh,
        in_specs=(
            P(None, ("groups", "learner"), None),
            P(),
            P(("groups", "learner")),
            P(None, ("groups", "learner"), "tensor", None),
            P(None, "tensor"),
            P(None, None, "tensor"),
            P("tensor", None),
            P(("groups", "learner", "tensor"), None),
            P(("groups", "learner"), "tensor"),
            P(None, ("groups", "learner"), "tensor"),
        ),
        out_specs=(
            P(None, ("groups", "learner"), None),
            P("groups", "tensor"),
            P(None, "groups", "tensor"),
        ),
        check_vma=False,
    )
```
